32 devices in a mesh: gx: 8 (over z, y), gy: 4 (over x, core).
Axes of the slice: x: 2, y: 2, z: 4, core: 2. Of those that a mesh axis runs over, the one named last changes fastest.
Arguments:
- saved_fractions: float32 [8, 16, 128, 512], P(None, None, 'gx', 'gy'), may hold values from 0 to 1
- adjoint_seed: bfloat16 [8, 16, 128, 512], P(None, None, 'gx', 'gy'), may hold values from -6 to 6
- slot_ids: int32 [8, 128, 512], P(None, 'gx', 'gy'), may hold values from 0 to 255, as said below
- active_counts: int32 [128, 512], P('gx', 'gy'), may hold values from 1 to 8
- mobility: float32 [256], replicated, may hold values from 0.5 to 2
- owner_pos: int32 [256], replicated, may hold values from 0 to 255, each once
- saved_instant: int32 [1], replicated, may hold values from 0 to 999
Outputs:
- phase_adjoint: float32 [8, 16, 128, 512], P(None, None, 'gx', 'gy')
- grain_gradient: float32 [256], P(('gx', 'gy'))
The draws below stay inside these ranges and needn't reach their ends.
Inputs may be any that keep to these rules, and one draw needn't show every extreme that they name: `slot_ids`: the 8 ids of a column are distinct, and every grain is the first slot's grain of some column.
All inputs are finite; a program needn't handle non-finite values.
Results may differ from the reference program's by a relative error of at most 0.0005.
Values sent between devices are 32-bit elements; how exact they have to be, the bound alone decides.
A program may use at most 192 MiB of HBM per device.

```python
import math
import jax
import jax.numpy as jnp
from jax import lax

K = 8
TILE = 16
EXPLICIT_UPDATES = 4
CZ = 16
NX = 128
NY = 512
GRAINS = 256


NEAR_OFFSETS = ((0, 0), (1, 0), (0, 1), (1, 1))


def draw_slot_ids(key, part):
    key = jax.random.fold_in(key, 11)
    key_order, key_far, key_base = jax.random.split(key, 3)
    tiles_x = NX // TILE
    tiles_y = NY // TILE
    order = jax.random.permutation(key_order, tiles_x * tiles_y).astype(jnp.int32)
    xs = jnp.arange(NX, dtype=jnp.int32)
    ys = jnp.arange(NY, dtype=jnp.int32)
    tile_x = xs // TILE
    tile_y = ys // TILE
    side_x = jnp.where(xs % TILE >= TILE // 2, 1, -1).astype(jnp.int32)
    side_y = jnp.where(ys % TILE >= TILE // 2, 1, -1).astype(jnp.int32)
    stacked = []
    for off_x, off_y in NEAR_OFFSETS:
        near_x = (tile_x + off_x * side_x) % tiles_x
        near_y = (tile_y + off_y * side_y) % tiles_y
        stacked.append(order[near_x[:, None] * tiles_y + near_y[None, :]])
    far_x = jax.random.randint(key_far, (4, NX, NY), 2, tiles_x - 1, dtype=jnp.int32)
    base_y = jax.random.randint(key_base, (NX, NY), 0, tiles_y, dtype=jnp.int32)
    for extra in range(4):
        away_x = (tile_x[:, None] + far_x[extra]) % tiles_x
        away_y = (tile_y[None, :] + base_y + extra) % tiles_y
        stacked.append(order[away_x * tiles_y + away_y])
    return jnp.stack(stacked).astype(jnp.int32)


def draw_active_counts(key, part):
    key = jax.random.fold_in(key, 23)
    xs = jnp.arange(NX, dtype=jnp.int32) % TILE
    ys = jnp.arange(NY, dtype=jnp.int32) % TILE
    edge_x = jnp.minimum(xs, TILE - 1 - xs)
    edge_y = jnp.minimum(ys, TILE - 1 - ys)
    nearest = jnp.minimum(edge_x[:, None], edge_y[None, :])
    jitter = jax.random.randint(key, (NX, NY), 0, 2, dtype=jnp.int32)
    return jnp.clip(K - nearest - jitter, 1, K).astype(jnp.int32)


def shard_levels(rng, dims, cuts, low, high):
    def one(position, parts):
        draws = jax.random.uniform(jax.random.fold_in(jax.random.fold_in(rng, 6), position), (parts,), jnp.float32, low / len(cuts), high / len(cuts))
        return jnp.repeat(jnp.exp(draws), dims[position] // parts).reshape((-1,) + (1,) * (len(dims) - position - 1))

    loudness = one(*cuts[0])
    for cut in cuts[1:]:
        loudness = loudness * one(*cut)
    return loudness


def noise(stream_key, shape, deviation, limit, cuts=(), kind=jnp.bfloat16):
    array = deviation * jax.random.normal(stream_key, shape, jnp.float32)
    if cuts:
        array = array * shard_levels(stream_key, shape, cuts, -0.22, 0.18)
    return jnp.clip(array, -limit, limit).astype(kind)


def setup_inputs(seed: int = 0) -> dict:
    streams_of = jax.random.split(jax.random.key(seed), 8)
    return {
        "saved_fractions": jnp.clip(1.0 * jax.random.uniform(streams_of[0], (K, CZ, NX, NY), jnp.float32) ** shard_levels(streams_of[0], (K, CZ, NX, NY), ((2, 8), (3, 4)), -0.2, 0.2), 0.0, 1.0),
        "adjoint_seed": noise(streams_of[1], (K, CZ, NX, NY), 1.0, 6.0, ((2, 8), (3, 4))),
        "slot_ids": draw_slot_ids(jax.random.fold_in(streams_of[7], 71), 0),
        "active_counts": draw_active_counts(jax.random.fold_in(streams_of[7], 71), 0),
        "mobility": jnp.clip(jnp.exp(jax.random.uniform(streams_of[4], (GRAINS,), jnp.float32, math.log(0.5), math.log(2.0))), 0.5, 2.0),
        "owner_pos": jax.random.permutation(streams_of[5], GRAINS).astype(jnp.int32),
        "saved_instant": jax.random.randint(streams_of[6], (1,), 0, 1000).astype(jnp.int32),
    }


DT = 0.05
C_WELL = 1.0
C_PAIR = 0.25
OFFSETS = ((0, 1), (2, 1), (1, 0), (1, 2))

def thermal_map(saved_instant, update_interval):
    return 0.75 + 0.5 * jnp.cos(0.3 * (saved_instant[0].astype(jnp.float32) + update_interval))

def neighbor_matches(live_pad):
    width_a = live_pad.shape[1] - 2
    width_b = live_pad.shape[2] - 2
    centre = live_pad[:, 1:width_a + 1, 1:width_b + 1]
    result = []
    for dx, dy in OFFSETS:
        beside = live_pad[:, dx:dx + width_a, dy:dy + width_b]
        result.append(centre[:, None] == beside[None, :])
    return result

def update_fractions(phase_pad, crystal_equality, present_crystals, moving_crystals, factor):
    width_a = present_crystals.shape[1]
    width_b = present_crystals.shape[2]
    centre = phase_pad[:, :, 1:width_a + 1, 1:width_b + 1]
    total = jnp.zeros_like(centre)
    for index, (dx, dy) in enumerate(OFFSETS):
        beside = phase_pad[:, :, dx:dx + width_a, dy:dy + width_b]
        for slot in range(beside.shape[0]):
            total = total + jnp.where(crystal_equality[index][:, slot][:, None], beside[slot][None], 0.0)
    above = jnp.concatenate([centre[:, 1:], centre[:, -1:]], axis=1)
    below = jnp.concatenate([centre[:, :1], centre[:, :-1]], axis=1)
    laplace = total + above + below - 6.0 * centre
    occupied = lax.optimization_barrier(jnp.sum(centre * present_crystals[:, None], axis=0))
    drive = laplace + C_WELL * centre * (1.0 - centre) * (centre - 0.5) - C_PAIR * centre * (occupied[None] - centre)
    return centre + DT * factor * (present_crystals * moving_crystals)[:, None] * drive

def reference(saved_fractions, adjoint_seed, slot_ids, active_counts, mobility, owner_pos, saved_instant):
    slots = slot_ids.shape[0]
    slot_index = jnp.arange(slots, dtype=jnp.int32)[:, None, None]
    live = jnp.where(slot_index < active_counts[None], slot_ids, -1).astype(jnp.int32)
    present_crystals = (live >= 0).astype(jnp.float32)
    live_pad = jnp.pad(live, ((0, 0), (1, 1), (1, 1)), mode='wrap')
    crystal_equality = neighbor_matches(live_pad)

    def forward(start_phase, table):
        moving_crystals = table[slot_ids]
        order_parameter = start_phase * present_crystals[:, None]
        for update_interval in range(EXPLICIT_UPDATES):
            sweep_interval = jnp.pad(order_parameter, ((0, 0), (0, 0), (1, 1), (1, 1)), mode='wrap')
            order_parameter = jax.checkpoint(update_fractions)(sweep_interval, crystal_equality, present_crystals, moving_crystals, thermal_map(saved_instant, update_interval))
        return order_parameter
    _, pull = jax.vjp(forward, saved_fractions, mobility)
    phase_adjoint, grain_grad = pull(adjoint_seed.astype(saved_fractions.dtype))
    owned = jnp.zeros_like(grain_grad).at[owner_pos].set(grain_grad)
    return (phase_adjoint, owned)
```

```python
import functools

import jax
import jax.numpy as jnp
from jax import lax
from jax.experimental import pallas as pl
from jax.experimental.pallas import tpu as pltpu
from jax.sharding import PartitionSpec as P

STEPS = 4
MESH = pl.DeviceIdType.MESH
LANES = 128
EXCHANGES = 7


def take_rows(values, index):
    return jnp.take_along_axis(values, index, axis=0)


def lookup(tables, ids):
    row = lax.shift_right_logical(ids, 7)
    col = lax.bitwise_and(ids, 127)
    found = None
    for r, table in enumerate(tables):
        got = jnp.take_along_axis(table, col, axis=1)
        found = got if found is None else jnp.where(row == r, got, found)
    return found


def kernel(
    nx, ny, slots, depth, rows, out_per,
    therm, sf, seed, ids, counts, mob, opos,
    out, gout,
    p0, p1, p2, p3, a4, a3, a2, a1, drive0, seed32,
    live, index, match, moba, act, pos, gacc, ones,
    xh, ye, yh, hc, le, lxh, lyh,
    gs, g3, r1, s2, r2,
    xs_sem, xr_sem, ys_sem, yr_sem, ls_sem, lr_sem, s1_sem, q1_sem, s2_sem, q2_sem,
):
    gx = lax.axis_index("gx")
    gy = lax.axis_index("gy")
    ndev = nx * ny
    per = LANES // (2 * depth)
    packs = rows // per
    stride = depth * rows
    phases = (p0, p1, p2, p3)
    adjoints = {4: a4, 3: a3, 2: a2, 1: a1}

    barrier = pltpu.get_barrier_semaphore()
    for o in range(1, nx):
        pl.semaphore_signal(barrier, inc=1, device_id=(lax.rem(gx + o, nx), gy), device_id_type=MESH)
    for o in range(1, ny):
        pl.semaphore_signal(barrier, inc=1, device_id=(gx, lax.rem(gy + o, ny)), device_id_type=MESH)

    low_x = (lax.rem(gx + nx - 1, nx), gy)
    high_x = (lax.rem(gx + 1, nx), gy)
    low_y = (gx, lax.rem(gy + ny - 1, ny))
    high_y = (gx, lax.rem(gy + 1, ny))

    lane = lax.broadcasted_iota(jnp.int32, (slots, LANES), 1)
    sub = lax.broadcasted_iota(jnp.int32, (slots, LANES), 0)
    pair = lax.shift_right_logical(lane, 1)
    group = lane // (2 * depth)
    first = lane == 0
    final = lane == LANES - 1
    even = lax.bitwise_and(lane, 1) == 0

    def x_copies(e, src):
        return (
            pltpu.make_async_remote_copy(
                src_ref=src.at[rows - 1], dst_ref=xh.at[e, 0], send_sem=xs_sem.at[e, 0],
                recv_sem=xr_sem.at[e, 0], device_id=high_x, device_id_type=MESH),
            pltpu.make_async_remote_copy(
                src_ref=src.at[0], dst_ref=xh.at[e, 1], send_sem=xs_sem.at[e, 1],
                recv_sem=xr_sem.at[e, 1], device_id=low_x, device_id_type=MESH),
        )

    def y_copies(e):
        return (
            pltpu.make_async_remote_copy(
                src_ref=ye.at[e], dst_ref=yh.at[e, 0], send_sem=ys_sem.at[e, 0],
                recv_sem=yr_sem.at[e, 0], device_id=high_y, device_id_type=MESH),
            pltpu.make_async_remote_copy(
                src_ref=ye.at[e], dst_ref=yh.at[e, 1], send_sem=ys_sem.at[e, 1],
                recv_sem=yr_sem.at[e, 1], device_id=low_y, device_id_type=MESH),
        )

    def swap_sides(from_low, from_high):
        return jnp.where(even, pltpu.roll(from_high, LANES - 1, 1), pltpu.roll(from_low, 1, 1))

    def pack_row(e, x, values):
        packed = jnp.zeros((slots, LANES), jnp.float32)
        for z, value in enumerate(values):
            packed = jnp.where(pair == z, pltpu.roll(value, 2 * z + 1, 1), packed)
        part = lax.rem(x, per)
        packed = pltpu.roll(packed, part * (2 * depth), 1)
        ye[e, x // per] = jnp.where(group == part, packed, ye[e, x // per])

    mob_tables = [jnp.broadcast_to(mob[r : r + 1, :], (slots, LANES)) for r in range(mob.shape[0])]
    pos_tables = [jnp.broadcast_to(opos[r : r + 1, :], (slots, LANES)) for r in range(opos.shape[0])]
    edge = jnp.zeros((slots, LANES), jnp.int32)
    for x in range(rows):
        own = ids[pl.ds(x, slots, stride=rows), :]
        alive = sub < jnp.broadcast_to(counts[x : x + 1, :], (slots, LANES))
        here = jnp.where(alive, own, -1)
        live[x + 1] = here
        edge = jnp.where(pair == x, pltpu.roll(here, 2 * x + 1, 1), edge)
        active = jnp.where(alive, 1.0, 0.0)
        act[x] = active
        moba[x] = 0.05 * active * lookup(mob_tables, own)
        pos[x] = lookup(pos_tables, own)
        gacc[x] = jnp.zeros((slots, LANES), jnp.float32)
    le[...] = edge
    ye[...] = jnp.zeros(ye.shape, jnp.float32)
    span = slots * depth
    ones[...] = jnp.where(
        lax.broadcasted_iota(jnp.int32, (span, span), 0) // slots
        == lax.broadcasted_iota(jnp.int32, (span, span), 1) // slots,
        0.25, 0.0,
    ).astype(jnp.bfloat16)

    def load_phase(x, carry):
        active = act[x]
        values = []
        for z in range(depth):
            value = sf[pl.ds(z * rows + x, slots, stride=stride), :] * active
            p0[x, z] = value
            values.append(value)
        pack_row(0, x, values)
        return carry

    lax.fori_loop(0, rows, load_phase, 0)

    pl.semaphore_wait(barrier, (nx - 1) + (ny - 1))
    id_copies = (
        pltpu.make_async_remote_copy(
            src_ref=live.at[rows], dst_ref=lxh.at[0], send_sem=ls_sem.at[0],
            recv_sem=lr_sem.at[0], device_id=high_x, device_id_type=MESH),
        pltpu.make_async_remote_copy(
            src_ref=live.at[1], dst_ref=lxh.at[1], send_sem=ls_sem.at[1],
            recv_sem=lr_sem.at[1], device_id=low_x, device_id_type=MESH),
        pltpu.make_async_remote_copy(
            src_ref=le, dst_ref=lyh.at[0], send_sem=ls_sem.at[2],
            recv_sem=lr_sem.at[2], device_id=high_y, device_id_type=MESH),
        pltpu.make_async_remote_copy(
            src_ref=le, dst_ref=lyh.at[1], send_sem=ls_sem.at[3],
            recv_sem=lr_sem.at[3], device_id=low_y, device_id_type=MESH),
    )
    sent = list(id_copies)

    def launch(e, src):
        xc, yc = x_copies(e, src), y_copies(e)
        for c in yc + xc:
            c.start()
            sent.append(c)
        return xc, yc

    for c in id_copies:
        c.start()
    flight = {0: launch(0, p0)}

    def widen(i, carry):
        block = pl.ds(pl.multiple_of(i * 128, 128), 128)
        seed32[block, :] = seed[block, :].astype(jnp.float32)
        return carry

    lax.fori_loop(0, seed.shape[0] // 128, widen, 0)

    def load_seed(x, carry):
        active = act[x]
        values = []
        for z in range(depth):
            value = seed32[pl.ds(z * rows + x, slots, stride=stride), :] * active
            a4[x, z] = value
            values.append(value)
        pack_row(3, x, values)
        return carry

    lax.fori_loop(0, rows, load_seed, 0)
    flight[3] = launch(3, a4)

    for c in id_copies:
        c.wait_recv()
    live[0] = lxh[0]
    live[rows + 1] = lxh[1]
    id_sides = swap_sides(lyh[0], lyh[1])

    def match_row(x, carry):
        own = live[x + 1]
        side = pltpu.roll(id_sides, LANES - 1 - 2 * x, 1)
        beside = (
            live[x],
            live[x + 2],
            jnp.where(first, side, pltpu.roll(own, 1, 1)),
            jnp.where(final, side, pltpu.roll(own, LANES - 1, 1)),
        )
        for n, other in enumerate(beside):
            where = jnp.zeros((slots, LANES), jnp.int32)
            hit = jnp.zeros((slots, LANES), jnp.float32)
            for j in range(slots):
                same = own == jnp.broadcast_to(other[j : j + 1, :], (slots, LANES))
                where = jnp.where(same, j, where)
                hit = jnp.where(same, 1.0, hit)
            index[n, x] = where
            match[n, x] = hit
        return carry

    lax.fori_loop(0, rows, match_row, 0)

    def open_sides(e):
        for c in flight[e][1]:
            c.wait_recv()
        for i in range(packs):
            hc[e, i] = swap_sides(yh[e, 0, i], yh[e, 1, i])

    def lateral(e, x, centre, up, down):
        part = lax.rem(x, per)
        side_row = pltpu.roll(hc[e, x // per], lax.rem(LANES - part * (2 * depth), LANES), 1)
        where = [index[n, x] for n in range(4)]
        hit = [match[n, x] for n in range(4)]
        totals = []
        for z in range(depth):
            c = centre[z]
            side = pltpu.roll(side_row, LANES - 1 - 2 * z, 1)
            left = jnp.where(first, side, pltpu.roll(c, 1, 1))
            right = jnp.where(final, side, pltpu.roll(c, LANES - 1, 1))
            total = (
                take_rows(up(z), where[0]) * hit[0]
                + take_rows(down(z), where[1]) * hit[1]
                + take_rows(left, where[2]) * hit[2]
                + take_rows(right, where[3]) * hit[3]
            )
            total = total + centre[min(z + 1, depth - 1)] + centre[max(z - 1, 0)]
            totals.append(total)
        return totals

    def slot_sums(values):
        stacked = jnp.concatenate(values, axis=0).astype(jnp.bfloat16)
        sums = jnp.dot(ones[...], stacked, preferred_element_type=jnp.float32)
        return [sums[z * slots : (z + 1) * slots] for z in range(depth)]

    def forward_row(s, x, up, down):
        src, dst = phases[s], phases[s + 1]
        centre = [src[x, z] for z in range(depth)]
        rate = therm[s] * moba[x]
        crowd = slot_sums(centre)
        totals = lateral(s, x, centre, up, down)
        values = []
        for z in range(depth):
            c = centre[z]
            drive = totals[z] + c * ((1.75 - c) * c - (6.5 + crowd[z]))
            if s == 0:
                drive0[x, z] = drive
            value = c + rate * drive
            dst[x, z] = value
            values.append(value)
        if s + 1 < STEPS - 1:
            pack_row(s + 1, x, values)

    def backward_row(s, x, up, down):
        src, phase = adjoints[s + 1], phases[s]
        e = 3 + (STEPS - 1 - s)
        active = act[x]
        rate = therm[s] * moba[x]
        centre = [src[x, z] for z in range(depth)]
        c = [phase[x, z] for z in range(depth)]
        crowd = slot_sums(c)
        shared = slot_sums([rate * centre[z] * c[z] for z in range(depth)])
        totals = lateral(e, x, centre, up, down)
        values = []
        now = jnp.zeros((slots, LANES), jnp.float32)
        before = jnp.zeros((slots, LANES), jnp.float32)
        for z in range(depth):
            a = centre[z]
            spread = totals[z] - 6.0 * a
            local = (3.5 - 3.0 * c[z]) * c[z] - (0.5 + crowd[z])
            value = a + rate * (spread + a * local) - active * shared[z]
            if s > 0:
                adjoints[s][x, z] = value
                values.append(value)
                now = now + c[z] * (spread + a * ((1.75 - c[z]) * c[z] - (0.5 + crowd[z])))
                if s == 1:
                    before = before + value * drive0[x, z]
            else:
                out[pl.ds(z * rows + x, slots, stride=stride), :] = value
        if s > 0:
            gained = gacc[x] + therm[s] * now
            if s == 1:
                gained = gained + therm[0] * before
            gacc[x] = gained
            pack_row(e + 1, x, values)

    def inner(row, s, src):
        def body(x, carry):
            row(s, x, lambda z: src[x - 1, z], lambda z: src[x + 1, z])
            return carry

        lax.fori_loop(1, rows - 1, body, 0)

    def rim(row, s, src, e):
        for c in flight[e][0]:
            c.wait_recv()

        def top(z):
            return xh[e, 0, z]

        def bottom(z):
            return xh[e, 1, z]

        def body(i, carry):
            x = i * (rows - 1)
            low = i == 0

            def up(z):
                return jnp.where(low, xh[e, 0, z], src[rows - 2, z])

            def down(z):
                return jnp.where(low, src[1, z], xh[e, 1, z])

            row(s, x, up, down)
            return carry

        lax.fori_loop(0, 2, body, 0)

    for s in range(STEPS - 1):
        open_sides(s)
        inner(forward_row, s, phases[s])
        rim(forward_row, s, phases[s], s)
        if s + 1 < STEPS - 1:
            flight[s + 1] = launch(s + 1, phases[s + 1])

    for s in range(STEPS - 1, 0, -1):
        e = 3 + (STEPS - 1 - s)
        open_sides(e)
        inner(backward_row, s, adjoints[s + 1])
        rim(backward_row, s, adjoints[s + 1], e)
        flight[e + 1] = launch(e + 1, adjoints[s])

    which = lax.broadcasted_iota(jnp.int32, (ndev, LANES), 0)

    def gather_grains(x, total):
        value = 0.05 * gacc[x]
        spot = pos[x]
        owner = spot // out_per
        place = spot - owner * out_per
        picks, terms = [], []
        for k in range(slots):
            picks.append(jnp.where(which == jnp.broadcast_to(owner[k : k + 1, :], (ndev, LANES)), 1.0, 0.0))
            term = jnp.where(
                sub == jnp.broadcast_to(place[k : k + 1, :], (slots, LANES)),
                jnp.broadcast_to(value[k : k + 1, :], (slots, LANES)), 0.0)
            coarse = term.astype(jnp.bfloat16).astype(jnp.float32)
            terms.append(jnp.concatenate([coarse, term - coarse], axis=0))
        pick = jnp.concatenate(picks, axis=1).astype(jnp.bfloat16)
        term = jnp.concatenate(terms, axis=1).astype(jnp.bfloat16)
        return total + lax.dot_general(
            pick, term, (((1,), (1,)), ((), ())), preferred_element_type=jnp.float32)

    total = lax.fori_loop(0, rows, gather_grains, jnp.zeros((ndev, 2 * slots), jnp.float32))
    gs[...] = jnp.zeros(gs.shape, jnp.float32)
    gs[:, 0 : 2 * slots] = total
    for d in range(ndev):
        g3[d] = gs[d : d + 1, :]
    stage1 = []
    for o in range(1, nx):
        to = lax.rem(gx + o, nx)
        c = pltpu.make_async_remote_copy(
            src_ref=g3.at[pl.ds(to * ny, ny)], dst_ref=r1.at[o], send_sem=s1_sem.at[o],
            recv_sem=q1_sem.at[o], device_id=(to, gy), device_id_type=MESH)
        c.start()
        stage1.append(c)
        sent.append(c)

    open_sides(EXCHANGES - 1)
    inner(backward_row, 0, a1)

    for c in stage1:
        c.wait_recv()
    summed = g3[pl.ds(gx * ny, ny)]
    for o in range(1, nx):
        summed = summed + r1[o]
    s2[...] = summed
    stage2 = []
    for o in range(1, ny):
        to = lax.rem(gy + o, ny)
        c = pltpu.make_async_remote_copy(
            src_ref=s2.at[to], dst_ref=r2.at[o], send_sem=s2_sem.at[o],
            recv_sem=q2_sem.at[o], device_id=(gx, to), device_id_type=MESH)
        c.start()
        stage2.append(c)
        sent.append(c)

    rim(backward_row, 0, a1, EXCHANGES - 1)

    for c in stage2:
        c.wait_recv()
    whole = s2[gy]
    for o in range(1, ny):
        whole = whole + r2[o]
    gout[...] = whole + pltpu.roll(whole, LANES - slots, 1)
    for c in sent:
        c.wait_send()


def shards(
    nx, ny,
    saved_fractions, adjoint_seed, slot_ids, active_counts, mobility, owner_pos, saved_instant
):
    slots, depth, rows, cols = saved_fractions.shape
    grains = mobility.shape[0]
    ndev = nx * ny
    out_per = grains // ndev
    steps = jnp.arange(STEPS, dtype=jnp.float32)
    therm = 0.75 + 0.5 * jnp.cos(0.3 * (saved_instant[0].astype(jnp.float32) + steps))
    flat = slots * depth * rows
    block = pltpu.VMEM((rows, depth, slots, cols), jnp.float32)
    plane = pltpu.VMEM((rows, slots, cols), jnp.float32)
    packs = rows * 2 * depth // LANES
    dma = pltpu.SemaphoreType.DMA
    vmem = pl.BlockSpec(memory_space=pltpu.VMEM)
    adjoint, owned = pl.pallas_call(
        functools.partial(kernel, nx, ny, slots, depth, rows, out_per),
        out_shape=(
            jax.ShapeDtypeStruct((flat, cols), jnp.float32),
            jax.ShapeDtypeStruct((1, LANES), jnp.float32),
        ),
        in_specs=[pl.BlockSpec(memory_space=pltpu.SMEM)] + [vmem] * 6,
        out_specs=(vmem, vmem),
        scratch_shapes=[block] * 9 + [
            pltpu.VMEM((flat, cols), jnp.float32),
            pltpu.VMEM((rows + 2, slots, cols), jnp.int32),
            pltpu.VMEM((4, rows, slots, cols), jnp.int32),
            pltpu.VMEM((4, rows, slots, cols), jnp.float32),
            plane, plane,
            pltpu.VMEM((rows, slots, cols), jnp.int32),
            plane,
            pltpu.VMEM((slots * depth, slots * depth), jnp.bfloat16),
            pltpu.VMEM((EXCHANGES, 2, depth, slots, cols), jnp.float32),
            pltpu.VMEM((EXCHANGES, packs, slots, LANES), jnp.float32),
            pltpu.VMEM((EXCHANGES, 2, packs, slots, LANES), jnp.float32),
            pltpu.VMEM((EXCHANGES, packs, slots, LANES), jnp.float32),
            pltpu.VMEM((slots, LANES), jnp.int32),
            pltpu.VMEM((2, slots, LANES), jnp.int32),
            pltpu.VMEM((2, slots, LANES), jnp.int32),
            pltpu.VMEM((ndev, LANES), jnp.float32),
            pltpu.VMEM((ndev, 1, LANES), jnp.float32),
            pltpu.VMEM((nx, ny, 1, LANES), jnp.float32),
            pltpu.VMEM((ny, 1, LANES), jnp.float32),
            pltpu.VMEM((ny, 1, LANES), jnp.float32),
            dma((EXCHANGES, 2)), dma((EXCHANGES, 2)),
            dma((EXCHANGES, 2)), dma((EXCHANGES, 2)),
            dma((4,)), dma((4,)),
            dma((nx,)), dma((nx,)), dma((ny,)), dma((ny,)),
        ],
        compiler_params=pltpu.CompilerParams(
            collective_id=0, has_side_effects=True, vmem_limit_bytes=48 * 1024 * 1024
        ),
    )(
        therm,
        saved_fractions.reshape(flat, cols),
        adjoint_seed.reshape(flat, cols),
        slot_ids.reshape(slots * rows, cols),
        active_counts,
        mobility.reshape(grains // LANES, LANES),
        owner_pos.reshape(grains // LANES, LANES),
    )
    return adjoint.reshape(saved_fractions.shape), owned[0, :out_per]


def solution(mesh):
    placed = (
        P(None, None, "gx", "gy"),
        P(None, None, "gx", "gy"),
        P(None, "gx", "gy"),
        P("gx", "gy"),
        P(),
        P(),
        P(),
    )
    return jax.shard_map(
        functools.partial(shards, mesh.shape["gx"], mesh.shape["gy"]),
        mesh=mesh,
        in_specs=placed,
        out_specs=(P(None, None, "gx", "gy"), P(("gx", "gy"))),
        check_vma=False,
    )
```

```python
import functools

import jax
import jax.numpy as jnp
from jax import lax
from jax.experimental import pallas as pl
from jax.experimental.pallas import tpu as pltpu
from jax.sharding import PartitionSpec as P

STEPS = 4
MESH = pl.DeviceIdType.MESH
LANES = 128
EXCHANGES = 7


def take_rows(values, index):
    return jnp.take_along_axis(values, index, axis=0)


def lookup(tables, ids):
    row = lax.shift_right_logical(ids, 7)
    col = lax.bitwise_and(ids, 127)
    found = None
    for r, table in enumerate(tables):
        got = jnp.take_along_axis(table, col, axis=1)
        found = got if found is None else jnp.where(row == r, got, found)
    return found


def kernel(
    nx, ny, slots, depth, rows, out_per,
    therm, sf, seed, ids, counts, mob, opos,
    out, gout,
    p0, p1, p2, p3, a4, a3, a2, a1, drive0, seed32,
    live, index, match, moba, act, pos, gacc, ones,
    xh, ye, yh, hc, rim_rows, le, lxh, lyh,
    gs, g3, r1, s2, r2,
    xs_sem, xr_sem, ys_sem, yr_sem, ls_sem, lr_sem, s1_sem, q1_sem, s2_sem, q2_sem,
):
    gx = lax.axis_index("gx")
    gy = lax.axis_index("gy")
    ndev = nx * ny
    per = LANES // (2 * depth)
    packs = rows // per
    stride = depth * rows
    phases = (p0, p1, p2, p3)
    adjoints = {4: a4, 3: a3, 2: a2, 1: a1}

    barrier = pltpu.get_barrier_semaphore()
    for o in range(1, nx):
        pl.semaphore_signal(barrier, inc=1, device_id=(lax.rem(gx + o, nx), gy), device_id_type=MESH)
    for o in range(1, ny):
        pl.semaphore_signal(barrier, inc=1, device_id=(gx, lax.rem(gy + o, ny)), device_id_type=MESH)

    low_x = (lax.rem(gx + nx - 1, nx), gy)
    high_x = (lax.rem(gx + 1, nx), gy)
    low_y = (gx, lax.rem(gy + ny - 1, ny))
    high_y = (gx, lax.rem(gy + 1, ny))

    lane = lax.broadcasted_iota(jnp.int32, (slots, LANES), 1)
    sub = lax.broadcasted_iota(jnp.int32, (slots, LANES), 0)
    pair = lax.shift_right_logical(lane, 1)
    group = lane // (2 * depth)
    first = lane == 0
    final = lane == LANES - 1
    even = lax.bitwise_and(lane, 1) == 0

    def x_copies(e, src):
        return (
            pltpu.make_async_remote_copy(
                src_ref=src.at[rows - 1], dst_ref=xh.at[e, 0], send_sem=xs_sem.at[e, 0],
                recv_sem=xr_sem.at[e, 0], device_id=high_x, device_id_type=MESH),
            pltpu.make_async_remote_copy(
                src_ref=src.at[0], dst_ref=xh.at[e, 1], send_sem=xs_sem.at[e, 1],
                recv_sem=xr_sem.at[e, 1], device_id=low_x, device_id_type=MESH),
        )

    def y_copies(e):
        return (
            pltpu.make_async_remote_copy(
                src_ref=ye.at[e], dst_ref=yh.at[e, 0], send_sem=ys_sem.at[e, 0],
                recv_sem=yr_sem.at[e, 0], device_id=high_y, device_id_type=MESH),
            pltpu.make_async_remote_copy(
                src_ref=ye.at[e], dst_ref=yh.at[e, 1], send_sem=ys_sem.at[e, 1],
                recv_sem=yr_sem.at[e, 1], device_id=low_y, device_id_type=MESH),
        )

    def swap_sides(from_low, from_high):
        return jnp.where(even, pltpu.roll(from_high, LANES - 1, 1), pltpu.roll(from_low, 1, 1))

    def pack_row(e, x, values):
        packed = jnp.zeros((slots, LANES), jnp.float32)
        for z, value in enumerate(values):
            packed = jnp.where(pair == z, pltpu.roll(value, 2 * z + 1, 1), packed)
        rim_rows[e, x] = packed

    def fill_sides(e):
        for i in range(packs):
            whole = rim_rows[e, i * per]
            for part in range(1, per):
                turned = pltpu.roll(rim_rows[e, i * per + part], part * (2 * depth), 1)
                whole = jnp.where(group == part, turned, whole)
            ye[e, i] = whole

    def rows_in(start, stop, by, body):
        def several(i, carry):
            for q in range(by):
                body(start + i * by + q)
            return carry

        lax.fori_loop(0, (stop - start) // by, several, 0)

    mob_tables = [jnp.broadcast_to(mob[r : r + 1, :], (slots, LANES)) for r in range(mob.shape[0])]
    pos_tables = [jnp.broadcast_to(opos[r : r + 1, :], (slots, LANES)) for r in range(opos.shape[0])]
    edge = jnp.zeros((slots, LANES), jnp.int32)
    for x in range(rows):
        own = ids[pl.ds(x, slots, stride=rows), :]
        alive = sub < jnp.broadcast_to(counts[x : x + 1, :], (slots, LANES))
        here = jnp.where(alive, own, -1)
        live[x + 1] = here
        edge = jnp.where(pair == x, pltpu.roll(here, 2 * x + 1, 1), edge)
        active = jnp.where(alive, 1.0, 0.0)
        act[x] = active
        moba[x] = 0.05 * active * lookup(mob_tables, own)
        pos[x] = lookup(pos_tables, own)
        gacc[x] = jnp.zeros((slots, LANES), jnp.float32)
    le[...] = edge
    span = slots * depth
    ones[...] = jnp.where(
        lax.broadcasted_iota(jnp.int32, (span, span), 0) // slots
        == lax.broadcasted_iota(jnp.int32, (span, span), 1) // slots,
        0.25, 0.0,
    ).astype(jnp.bfloat16)

    def load_phase(x):
        active = act[x]
        values = []
        for z in range(depth):
            value = sf[pl.ds(z * rows + x, slots, stride=stride), :] * active
            p0[x, z] = value
            values.append(value)
        pack_row(0, x, values)

    rows_in(0, rows, 4, load_phase)

    pl.semaphore_wait(barrier, (nx - 1) + (ny - 1))
    id_copies = (
        pltpu.make_async_remote_copy(
            src_ref=live.at[rows], dst_ref=lxh.at[0], send_sem=ls_sem.at[0],
            recv_sem=lr_sem.at[0], device_id=high_x, device_id_type=MESH),
        pltpu.make_async_remote_copy(
            src_ref=live.at[1], dst_ref=lxh.at[1], send_sem=ls_sem.at[1],
            recv_sem=lr_sem.at[1], device_id=low_x, device_id_type=MESH),
        pltpu.make_async_remote_copy(
            src_ref=le, dst_ref=lyh.at[0], send_sem=ls_sem.at[2],
            recv_sem=lr_sem.at[2], device_id=high_y, device_id_type=MESH),
        pltpu.make_async_remote_copy(
            src_ref=le, dst_ref=lyh.at[1], send_sem=ls_sem.at[3],
            recv_sem=lr_sem.at[3], device_id=low_y, device_id_type=MESH),
    )
    sent = list(id_copies)

    def launch(e, src):
        fill_sides(e)
        xc, yc = x_copies(e, src), y_copies(e)
        for c in yc + xc:
            c.start()
            sent.append(c)
        return xc, yc

    for c in id_copies:
        c.start()
    flight = {0: launch(0, p0)}

    def widen(i, carry):
        block = pl.ds(pl.multiple_of(i * 128, 128), 128)
        seed32[block, :] = seed[block, :].astype(jnp.float32)
        return carry

    lax.fori_loop(0, seed.shape[0] // 128, widen, 0)

    def load_seed(x):
        active = act[x]
        values = []
        for z in range(depth):
            value = seed32[pl.ds(z * rows + x, slots, stride=stride), :] * active
            a4[x, z] = value
            values.append(value)
        pack_row(3, x, values)

    rows_in(0, rows, 4, load_seed)
    flight[3] = launch(3, a4)

    for c in id_copies:
        c.wait_recv()
    live[0] = lxh[0]
    live[rows + 1] = lxh[1]
    id_sides = swap_sides(lyh[0], lyh[1])

    def match_row(x):
        own = live[x + 1]
        side = pltpu.roll(id_sides, LANES - 1 - 2 * x, 1)
        beside = (
            live[x],
            live[x + 2],
            jnp.where(first, side, pltpu.roll(own, 1, 1)),
            jnp.where(final, side, pltpu.roll(own, LANES - 1, 1)),
        )
        for n, other in enumerate(beside):
            where = jnp.zeros((slots, LANES), jnp.int32)
            hit = jnp.zeros((slots, LANES), jnp.float32)
            for j in range(slots):
                same = own == jnp.broadcast_to(other[j : j + 1, :], (slots, LANES))
                where = jnp.where(same, j, where)
                hit = jnp.where(same, 1.0, hit)
            index[n, x] = where
            match[n, x] = hit

    rows_in(0, rows, 4, match_row)

    def open_sides(e):
        for c in flight[e][1]:
            c.wait_recv()
        for i in range(packs):
            sides = swap_sides(yh[e, 0, i], yh[e, 1, i])
            for part in range(per):
                hc[e, i * per + part] = pltpu.roll(sides, LANES - 1 - part * (2 * depth), 1)

    def lateral(e, x, centre, up, down):
        side_row = hc[e, x]
        where = [index[n, x] for n in range(4)]
        hit = [match[n, x] for n in range(4)]
        totals = []
        for z in range(depth):
            c = centre[z]
            side = side_row if z == 0 else pltpu.roll(side_row, LANES - 2 * z, 1)
            left = jnp.where(first, side, pltpu.roll(c, 1, 1))
            right = jnp.where(final, side, pltpu.roll(c, LANES - 1, 1))
            total = (
                take_rows(up(z), where[0]) * hit[0]
                + take_rows(down(z), where[1]) * hit[1]
                + take_rows(left, where[2]) * hit[2]
                + take_rows(right, where[3]) * hit[3]
            )
            total = total + centre[min(z + 1, depth - 1)] + centre[max(z - 1, 0)]
            totals.append(total)
        return totals

    def slot_sums(values):
        stacked = jnp.concatenate(values, axis=0).astype(jnp.bfloat16)
        sums = jnp.dot(ones[...], stacked, preferred_element_type=jnp.float32)
        return [sums[z * slots : (z + 1) * slots] for z in range(depth)]

    def forward_row(s, x, up, down):
        src, dst = phases[s], phases[s + 1]
        centre = [src[x, z] for z in range(depth)]
        rate = therm[s] * moba[x]
        crowd = slot_sums(centre)
        totals = lateral(s, x, centre, up, down)
        values = []
        for z in range(depth):
            c = centre[z]
            drive = totals[z] + c * ((1.75 - c) * c - (6.5 + crowd[z]))
            if s == 0:
                drive0[x, z] = drive
            value = c + rate * drive
            dst[x, z] = value
            values.append(value)
        if s + 1 < STEPS - 1:
            pack_row(s + 1, x, values)

    def backward_row(s, x, up, down):
        src, phase = adjoints[s + 1], phases[s]
        e = 3 + (STEPS - 1 - s)
        active = act[x]
        rate = therm[s] * moba[x]
        centre = [src[x, z] for z in range(depth)]
        c = [phase[x, z] for z in range(depth)]
        crowd = slot_sums(c)
        shared = slot_sums([rate * centre[z] * c[z] for z in range(depth)])
        totals = lateral(e, x, centre, up, down)
        values = []
        now = jnp.zeros((slots, LANES), jnp.float32)
        before = jnp.zeros((slots, LANES), jnp.float32)
        for z in range(depth):
            a = centre[z]
            spread = totals[z] - 6.0 * a
            local = (3.5 - 3.0 * c[z]) * c[z] - (0.5 + crowd[z])
            value = a + rate * (spread + a * local) - active * shared[z]
            if s > 0:
                adjoints[s][x, z] = value
                values.append(value)
                now = now + c[z] * (spread + a * ((1.75 - c[z]) * c[z] - (0.5 + crowd[z])))
                if s == 1:
                    before = before + value * drive0[x, z]
            else:
                out[pl.ds(z * rows + x, slots, stride=stride), :] = value
        if s > 0:
            gained = gacc[x] + therm[s] * now
            if s == 1:
                gained = gained + therm[0] * before
            gacc[x] = gained
            pack_row(e + 1, x, values)

    def inner(row, s, src):
        def body(x):
            row(s, x, lambda z: src[x - 1, z], lambda z: src[x + 1, z])

        rows_in(1, rows - 1, 2, body)

    def rim(row, s, src, e):
        for c in flight[e][0]:
            c.wait_recv()

        row(s, 0, lambda z: xh[e, 0, z], lambda z: src[1, z])
        row(s, rows - 1, lambda z: src[rows - 2, z], lambda z: xh[e, 1, z])

    for s in range(STEPS - 1):
        open_sides(s)
        inner(forward_row, s, phases[s])
        rim(forward_row, s, phases[s], s)
        if s + 1 < STEPS - 1:
            flight[s + 1] = launch(s + 1, phases[s + 1])

    for s in range(STEPS - 1, 0, -1):
        e = 3 + (STEPS - 1 - s)
        open_sides(e)
        inner(backward_row, s, adjoints[s + 1])
        rim(backward_row, s, adjoints[s + 1], e)
        flight[e + 1] = launch(e + 1, adjoints[s])

    which = lax.broadcasted_iota(jnp.int32, (ndev, LANES), 0)

    def gather_grains(x):
        value = 0.05 * gacc[x]
        spot = pos[x]
        owner = spot // out_per
        place = spot - owner * out_per
        picks, terms = [], []
        for k in range(slots):
            picks.append(jnp.where(which == jnp.broadcast_to(owner[k : k + 1, :], (ndev, LANES)), 1.0, 0.0))
            term = jnp.where(
                sub == jnp.broadcast_to(place[k : k + 1, :], (slots, LANES)),
                jnp.broadcast_to(value[k : k + 1, :], (slots, LANES)), 0.0)
            coarse = term.astype(jnp.bfloat16).astype(jnp.float32)
            terms.append(jnp.concatenate([coarse, term - coarse], axis=0))
        pick = jnp.concatenate(picks, axis=1).astype(jnp.bfloat16)
        term = jnp.concatenate(terms, axis=1).astype(jnp.bfloat16)
        return lax.dot_general(
            pick, term, (((1,), (1,)), ((), ())), preferred_element_type=jnp.float32)

    def gather_rows(i, total):
        for q in range(4):
            total = total + gather_grains(4 * i + q)
        return total

    total = lax.fori_loop(0, rows // 4, gather_rows, jnp.zeros((ndev, 2 * slots), jnp.float32))
    gs[...] = jnp.zeros(gs.shape, jnp.float32)
    gs[:, 0 : 2 * slots] = total
    for d in range(ndev):
        g3[d] = gs[d : d + 1, :]
    stage1 = []
    for o in range(1, nx):
        to = lax.rem(gx + o, nx)
        c = pltpu.make_async_remote_copy(
            src_ref=g3.at[pl.ds(to * ny, ny)], dst_ref=r1.at[o], send_sem=s1_sem.at[o],
            recv_sem=q1_sem.at[o], device_id=(to, gy), device_id_type=MESH)
        c.start()
        stage1.append(c)
        sent.append(c)

    open_sides(EXCHANGES - 1)
    inner(backward_row, 0, a1)

    for c in stage1:
        c.wait_recv()
    summed = g3[pl.ds(gx * ny, ny)]
    for o in range(1, nx):
        summed = summed + r1[o]
    s2[...] = summed
    stage2 = []
    for o in range(1, ny):
        to = lax.rem(gy + o, ny)
        c = pltpu.make_async_remote_copy(
            src_ref=s2.at[to], dst_ref=r2.at[o], send_sem=s2_sem.at[o],
            recv_sem=q2_sem.at[o], device_id=(gx, to), device_id_type=MESH)
        c.start()
        stage2.append(c)
        sent.append(c)

    rim(backward_row, 0, a1, EXCHANGES - 1)

    for c in stage2:
        c.wait_recv()
    whole = s2[gy]
    for o in range(1, ny):
        whole = whole + r2[o]
    gout[...] = whole + pltpu.roll(whole, LANES - slots, 1)
    for c in sent:
        c.wait_send()


def shards(
    nx, ny,
    saved_fractions, adjoint_seed, slot_ids, active_counts, mobility, owner_pos, saved_instant
):
    slots, depth, rows, cols = saved_fractions.shape
    grains = mobility.shape[0]
    ndev = nx * ny
    out_per = grains // ndev
    steps = jnp.arange(STEPS, dtype=jnp.float32)
    therm = 0.75 + 0.5 * jnp.cos(0.3 * (saved_instant[0].astype(jnp.float32) + steps))
    flat = slots * depth * rows
    block = pltpu.VMEM((rows, depth, slots, cols), jnp.float32)
    plane = pltpu.VMEM((rows, slots, cols), jnp.float32)
    packs = rows * 2 * depth // LANES
    dma = pltpu.SemaphoreType.DMA
    vmem = pl.BlockSpec(memory_space=pltpu.VMEM)
    adjoint, owned = pl.pallas_call(
        functools.partial(kernel, nx, ny, slots, depth, rows, out_per),
        out_shape=(
            jax.ShapeDtypeStruct((flat, cols), jnp.float32),
            jax.ShapeDtypeStruct((1, LANES), jnp.float32),
        ),
        in_specs=[pl.BlockSpec(memory_space=pltpu.SMEM)] + [vmem] * 6,
        out_specs=(vmem, vmem),
        scratch_shapes=[block] * 9 + [
            pltpu.VMEM((flat, cols), jnp.float32),
            pltpu.VMEM((rows + 2, slots, cols), jnp.int32),
            pltpu.VMEM((4, rows, slots, cols), jnp.int32),
            pltpu.VMEM((4, rows, slots, cols), jnp.float32),
            plane, plane,
            pltpu.VMEM((rows, slots, cols), jnp.int32),
            plane,
            pltpu.VMEM((slots * depth, slots * depth), jnp.bfloat16),
            pltpu.VMEM((EXCHANGES, 2, depth, slots, cols), jnp.float32),
            pltpu.VMEM((EXCHANGES, packs, slots, LANES), jnp.float32),
            pltpu.VMEM((EXCHANGES, 2, packs, slots, LANES), jnp.float32),
            pltpu.VMEM((EXCHANGES, rows, slots, LANES), jnp.float32),
            pltpu.VMEM((EXCHANGES, rows, slots, LANES), jnp.float32),
            pltpu.VMEM((slots, LANES), jnp.int32),
            pltpu.VMEM((2, slots, LANES), jnp.int32),
            pltpu.VMEM((2, slots, LANES), jnp.int32),
            pltpu.VMEM((ndev, LANES), jnp.float32),
            pltpu.VMEM((ndev, 1, LANES), jnp.float32),
            pltpu.VMEM((nx, ny, 1, LANES), jnp.float32),
            pltpu.VMEM((ny, 1, LANES), jnp.float32),
            pltpu.VMEM((ny, 1, LANES), jnp.float32),
            dma((EXCHANGES, 2)), dma((EXCHANGES, 2)),
            dma((EXCHANGES, 2)), dma((EXCHANGES, 2)),
            dma((4,)), dma((4,)),
            dma((nx,)), dma((nx,)), dma((ny,)), dma((ny,)),
        ],
        compiler_params=pltpu.CompilerParams(
            collective_id=0, has_side_effects=True, vmem_limit_bytes=48 * 1024 * 1024
        ),
    )(
        therm,
        saved_fractions.reshape(flat, cols),
        adjoint_seed.reshape(flat, cols),
        slot_ids.reshape(slots * rows, cols),
        active_counts,
        mobility.reshape(grains // LANES, LANES),
        owner_pos.reshape(grains // LANES, LANES),
    )
    return adjoint.reshape(saved_fractions.shape), owned[0, :out_per]


def solution(mesh):
    placed = (
        P(None, None, "gx", "gy"),
        P(None, None, "gx", "gy"),
        P(None, "gx", "gy"),
        P("gx", "gy"),
        P(),
        P(),
        P(),
    )
    return jax.shard_map(
        functools.partial(shards, mesh.shape["gx"], mesh.shape["gy"]),
        mesh=mesh,
        in_specs=placed,
        out_specs=(P(None, None, "gx", "gy"), P(("gx", "gy"))),
        check_vma=False,
    )
```

```python
import functools

import jax
import jax.numpy as jnp
from jax import lax
from jax.experimental import pallas as pl
from jax.experimental.pallas import tpu as pltpu
from jax.sharding import PartitionSpec as P

STEPS = 4
MESH = pl.DeviceIdType.MESH
LANES = 128
EXCHANGES = 7


def take_rows(values, index):
    return jnp.take_along_axis(values, index, axis=0)


def lookup(tables, ids):
    row = lax.shift_right_logical(ids, 7)
    col = lax.bitwise_and(ids, 127)
    found = None
    for r, table in enumerate(tables):
        got = jnp.take_along_axis(table, col, axis=1)
        found = got if found is None else jnp.where(row == r, got, found)
    return found


def kernel(
    nx, ny, slots, depth, rows, out_per,
    therm, sf, seed, ids, counts, mob, opos,
    out, gout,
    p0, p1, p2, p3, a4, a3, a2, a1, drive0, seed32,
    live, index, match, moba, act, pos, gacc, ones,
    xh, ye, yh, hc, rim_rows, le, lxh, lyh,
    gs, g3, r1, s2, r2,
    xs_sem, xr_sem, ys_sem, yr_sem, ls_sem, lr_sem, s1_sem, q1_sem, s2_sem, q2_sem,
):
    gx = lax.axis_index("gx")
    gy = lax.axis_index("gy")
    ndev = nx * ny
    per = LANES // (2 * depth)
    pieces = ((0, 2), (2, 4), (4, 5))
    cut = 1 + 2 * per
    used = [x for x in range(rows - 2)] + [4 * per, 4 * per + 1]
    stride = depth * rows
    phases = (p0, p1, p2, p3)
    adjoints = {4: a4, 3: a3, 2: a2, 1: a1}

    barrier = pltpu.get_barrier_semaphore()
    for o in range(1, nx):
        pl.semaphore_signal(barrier, inc=1, device_id=(lax.rem(gx + o, nx), gy), device_id_type=MESH)
    for o in range(1, ny):
        pl.semaphore_signal(barrier, inc=1, device_id=(gx, lax.rem(gy + o, ny)), device_id_type=MESH)

    low_x = (lax.rem(gx + nx - 1, nx), gy)
    high_x = (lax.rem(gx + 1, nx), gy)
    low_y = (gx, lax.rem(gy + ny - 1, ny))
    high_y = (gx, lax.rem(gy + 1, ny))

    lane = lax.broadcasted_iota(jnp.int32, (slots, LANES), 1)
    sub = lax.broadcasted_iota(jnp.int32, (slots, LANES), 0)
    pair = lax.shift_right_logical(lane, 1)
    group = lane // (2 * depth)
    first = lane == 0
    final = lane == LANES - 1
    even = lax.bitwise_and(lane, 1) == 0

    def x_copies(e, src):
        return (
            pltpu.make_async_remote_copy(
                src_ref=src.at[rows - 1], dst_ref=xh.at[e, 0], send_sem=xs_sem.at[e, 0],
                recv_sem=xr_sem.at[e, 0], device_id=high_x, device_id_type=MESH),
            pltpu.make_async_remote_copy(
                src_ref=src.at[0], dst_ref=xh.at[e, 1], send_sem=xs_sem.at[e, 1],
                recv_sem=xr_sem.at[e, 1], device_id=low_x, device_id_type=MESH),
        )

    def y_copies(e, p):
        block = pl.ds(pieces[p][0], pieces[p][1] - pieces[p][0])
        return [
            pltpu.make_async_remote_copy(
                src_ref=ye.at[e, block], dst_ref=yh.at[e, side, block], send_sem=ys_sem.at[e, p, side],
                recv_sem=yr_sem.at[e, p, side], device_id=target, device_id_type=MESH)
            for side, target in enumerate((high_y, low_y))
        ]

    def swap_sides(from_low, from_high):
        return jnp.where(even, pltpu.roll(from_high, LANES - 1, 1), pltpu.roll(from_low, 1, 1))

    def pack_row(e, slot, values):
        packed = jnp.zeros((slots, LANES), jnp.float32)
        for z, value in enumerate(values):
            packed = jnp.where(pair == z, pltpu.roll(value, 2 * z + 1, 1), packed)
        rim_rows[e, slot] = packed

    def fill_sides(e, p):
        for i in range(*pieces[p]):
            whole = rim_rows[e, i * per]
            for part in range(1, per):
                if i * per + part not in used:
                    continue
                turned = pltpu.roll(rim_rows[e, i * per + part], part * (2 * depth), 1)
                whole = jnp.where(group == part, turned, whole)
            ye[e, i] = whole

    def rows_in(start, stop, by, body):
        def several(i, carry):
            for q in range(by):
                body(start + i * by + q)
            return carry

        lax.fori_loop(0, (stop - start) // by, several, 0)

    mob_tables = [jnp.broadcast_to(mob[r : r + 1, :], (slots, LANES)) for r in range(mob.shape[0])]
    pos_tables = [jnp.broadcast_to(opos[r : r + 1, :], (slots, LANES)) for r in range(opos.shape[0])]
    edge = jnp.zeros((slots, LANES), jnp.int32)
    for x in range(rows):
        own = ids[pl.ds(x, slots, stride=rows), :]
        alive = sub < jnp.broadcast_to(counts[x : x + 1, :], (slots, LANES))
        here = jnp.where(alive, own, -1)
        live[x + 1] = here
        edge = jnp.where(pair == x, pltpu.roll(here, 2 * x + 1, 1), edge)
        active = jnp.where(alive, 1.0, 0.0)
        act[x] = active
        moba[x] = 0.05 * active * lookup(mob_tables, own)
        pos[x] = lookup(pos_tables, own)
        gacc[x] = jnp.zeros((slots, LANES), jnp.float32)
    le[...] = edge
    span = slots * depth
    ones[...] = jnp.where(
        lax.broadcasted_iota(jnp.int32, (span, span), 0) // slots
        == lax.broadcasted_iota(jnp.int32, (span, span), 1) // slots,
        0.25, 0.0,
    ).astype(jnp.bfloat16)

    def load_phase(x, slot):
        active = act[x]
        values = []
        for z in range(depth):
            value = sf[pl.ds(z * rows + x, slots, stride=stride), :] * active
            p0[x, z] = value
            values.append(value)
        pack_row(0, slot, values)

    rows_in(1, rows - 1, 2, lambda x: load_phase(x, x - 1))
    load_phase(0, 4 * per)
    load_phase(rows - 1, 4 * per + 1)

    pl.semaphore_wait(barrier, (nx - 1) + (ny - 1))
    id_copies = (
        pltpu.make_async_remote_copy(
            src_ref=live.at[rows], dst_ref=lxh.at[0], send_sem=ls_sem.at[0],
            recv_sem=lr_sem.at[0], device_id=high_x, device_id_type=MESH),
        pltpu.make_async_remote_copy(
            src_ref=live.at[1], dst_ref=lxh.at[1], send_sem=ls_sem.at[1],
            recv_sem=lr_sem.at[1], device_id=low_x, device_id_type=MESH),
        pltpu.make_async_remote_copy(
            src_ref=le, dst_ref=lyh.at[0], send_sem=ls_sem.at[2],
            recv_sem=lr_sem.at[2], device_id=high_y, device_id_type=MESH),
        pltpu.make_async_remote_copy(
            src_ref=le, dst_ref=lyh.at[1], send_sem=ls_sem.at[3],
            recv_sem=lr_sem.at[3], device_id=low_y, device_id_type=MESH),
    )
    sent = list(id_copies)

    flight = {}

    def launch_y(e, p):
        fill_sides(e, p)
        flight[e, p] = y_copies(e, p)
        for c in flight[e, p]:
            c.start()
            sent.append(c)

    def launch_x(e, src):
        flight[e, "x"] = x_copies(e, src)
        for c in flight[e, "x"]:
            c.start()
            sent.append(c)

    def launch(e, src):
        for p in range(len(pieces)):
            launch_y(e, p)
        launch_x(e, src)

    for c in id_copies:
        c.start()
    launch(0, p0)

    def widen(i, carry):
        block = pl.ds(pl.multiple_of(i * 128, 128), 128)
        seed32[block, :] = seed[block, :].astype(jnp.float32)
        return carry

    lax.fori_loop(0, seed.shape[0] // 128, widen, 0)

    def load_seed(x, slot):
        active = act[x]
        values = []
        for z in range(depth):
            value = seed32[pl.ds(z * rows + x, slots, stride=stride), :] * active
            a4[x, z] = value
            values.append(value)
        pack_row(3, slot, values)

    rows_in(1, rows - 1, 2, lambda x: load_seed(x, x - 1))
    load_seed(0, 4 * per)
    load_seed(rows - 1, 4 * per + 1)
    launch(3, a4)

    for c in id_copies:
        c.wait_recv()
    live[0] = lxh[0]
    live[rows + 1] = lxh[1]
    id_sides = swap_sides(lyh[0], lyh[1])

    def match_row(x):
        own = live[x + 1]
        side = pltpu.roll(id_sides, LANES - 1 - 2 * x, 1)
        beside = (
            live[x],
            live[x + 2],
            jnp.where(first, side, pltpu.roll(own, 1, 1)),
            jnp.where(final, side, pltpu.roll(own, LANES - 1, 1)),
        )
        for n, other in enumerate(beside):
            where = jnp.zeros((slots, LANES), jnp.int32)
            hit = jnp.zeros((slots, LANES), jnp.float32)
            for j in range(slots):
                same = own == jnp.broadcast_to(other[j : j + 1, :], (slots, LANES))
                where = jnp.where(same, j, where)
                hit = jnp.where(same, 1.0, hit)
            index[n, x] = where
            match[n, x] = hit

    rows_in(0, rows, 4, match_row)

    def open_sides(e, p):
        for c in flight[e, p]:
            c.wait_recv()
        for i in range(*pieces[p]):
            sides = swap_sides(yh[e, 0, i], yh[e, 1, i])
            for part in range(per):
                if i * per + part not in used:
                    continue
                hc[e, i * per + part] = pltpu.roll(sides, LANES - 1 - part * (2 * depth), 1)

    def lateral(e, x, slot, centre, up, down):
        side_row = hc[e, slot]
        where = [index[n, x] for n in range(4)]
        hit = [match[n, x] for n in range(4)]
        totals = []
        for z in range(depth):
            c = centre[z]
            side = side_row if z == 0 else pltpu.roll(side_row, LANES - 2 * z, 1)
            left = jnp.where(first, side, pltpu.roll(c, 1, 1))
            right = jnp.where(final, side, pltpu.roll(c, LANES - 1, 1))
            total = (
                take_rows(up(z), where[0]) * hit[0]
                + take_rows(down(z), where[1]) * hit[1]
                + take_rows(left, where[2]) * hit[2]
                + take_rows(right, where[3]) * hit[3]
            )
            total = total + centre[min(z + 1, depth - 1)] + centre[max(z - 1, 0)]
            totals.append(total)
        return totals

    def slot_sums(values):
        stacked = jnp.concatenate(values, axis=0).astype(jnp.bfloat16)
        sums = jnp.dot(ones[...], stacked, preferred_element_type=jnp.float32)
        return [sums[z * slots : (z + 1) * slots] for z in range(depth)]

    def forward_row(s, x, slot, up, down):
        src, dst = phases[s], phases[s + 1]
        centre = [src[x, z] for z in range(depth)]
        rate = therm[s] * moba[x]
        crowd = slot_sums(centre)
        totals = lateral(s, x, slot, centre, up, down)
        values = []
        for z in range(depth):
            c = centre[z]
            drive = totals[z] + c * ((1.75 - c) * c - (6.5 + crowd[z]))
            if s == 0:
                drive0[x, z] = drive
            value = c + rate * drive
            dst[x, z] = value
            values.append(value)
        if s + 1 < STEPS - 1:
            pack_row(s + 1, slot, values)

    def backward_row(s, x, slot, up, down):
        src, phase = adjoints[s + 1], phases[s]
        e = 3 + (STEPS - 1 - s)
        active = act[x]
        rate = therm[s] * moba[x]
        centre = [src[x, z] for z in range(depth)]
        c = [phase[x, z] for z in range(depth)]
        crowd = slot_sums(c)
        shared = slot_sums([rate * centre[z] * c[z] for z in range(depth)])
        totals = lateral(e, x, slot, centre, up, down)
        values = []
        now = jnp.zeros((slots, LANES), jnp.float32)
        before = jnp.zeros((slots, LANES), jnp.float32)
        for z in range(depth):
            a = centre[z]
            spread = totals[z] - 6.0 * a
            local = (3.5 - 3.0 * c[z]) * c[z] - (0.5 + crowd[z])
            value = a + rate * (spread + a * local) - active * shared[z]
            if s > 0:
                adjoints[s][x, z] = value
                values.append(value)
                now = now + c[z] * (spread + a * ((1.75 - c[z]) * c[z] - (0.5 + crowd[z])))
                if s == 1:
                    before = before + value * drive0[x, z]
            else:
                out[pl.ds(z * rows + x, slots, stride=stride), :] = value
        if s > 0:
            gained = gacc[x] + therm[s] * now
            if s == 1:
                gained = gained + therm[0] * before
            gacc[x] = gained
            pack_row(e + 1, slot, values)

    def inner(row, s, src, e, after):
        def body(x):
            row(s, x, x - 1, lambda z: src[x - 1, z], lambda z: src[x + 1, z])

        open_sides(e, 0)
        rows_in(1, cut, 2, body)
        if after is not None:
            launch_y(after, 0)
        open_sides(e, 1)
        rows_in(cut, rows - 1, 2, body)
        if after is not None:
            launch_y(after, 1)

    def rim(row, s, src, e):
        open_sides(e, 2)
        for c in flight[e, "x"]:
            c.wait_recv()
        row(s, 0, 4 * per, lambda z: xh[e, 0, z], lambda z: src[1, z])
        row(s, rows - 1, 4 * per + 1, lambda z: src[rows - 2, z], lambda z: xh[e, 1, z])

    for s in range(STEPS - 1):
        after = s + 1 if s + 1 < STEPS - 1 else None
        inner(forward_row, s, phases[s], s, after)
        rim(forward_row, s, phases[s], s)
        if after is not None:
            launch_x(after, phases[s + 1])
            launch_y(after, 2)

    for s in range(STEPS - 1, 0, -1):
        e = 3 + (STEPS - 1 - s)
        inner(backward_row, s, adjoints[s + 1], e, e + 1)
        rim(backward_row, s, adjoints[s + 1], e)
        launch_x(e + 1, adjoints[s])
        launch_y(e + 1, 2)

    which = lax.broadcasted_iota(jnp.int32, (ndev, LANES), 0)

    def gather_grains(x):
        value = 0.05 * gacc[x]
        spot = pos[x]
        owner = spot // out_per
        place = spot - owner * out_per
        picks, terms = [], []
        for k in range(slots):
            picks.append(jnp.where(which == jnp.broadcast_to(owner[k : k + 1, :], (ndev, LANES)), 1.0, 0.0))
            term = jnp.where(
                sub == jnp.broadcast_to(place[k : k + 1, :], (slots, LANES)),
                jnp.broadcast_to(value[k : k + 1, :], (slots, LANES)), 0.0)
            coarse = term.astype(jnp.bfloat16).astype(jnp.float32)
            terms.append(jnp.concatenate([coarse, term - coarse], axis=0))
        pick = jnp.concatenate(picks, axis=1).astype(jnp.bfloat16)
        term = jnp.concatenate(terms, axis=1).astype(jnp.bfloat16)
        return lax.dot_general(
            pick, term, (((1,), (1,)), ((), ())), preferred_element_type=jnp.float32)

    def gather_rows(i, total):
        for q in range(4):
            total = total + gather_grains(4 * i + q)
        return total

    total = lax.fori_loop(0, rows // 4, gather_rows, jnp.zeros((ndev, 2 * slots), jnp.float32))
    gs[...] = jnp.zeros(gs.shape, jnp.float32)
    gs[:, 0 : 2 * slots] = total
    for d in range(ndev):
        g3[d] = gs[d : d + 1, :]
    stage1 = []
    for o in range(1, nx):
        to = lax.rem(gx + o, nx)
        c = pltpu.make_async_remote_copy(
            src_ref=g3.at[pl.ds(to * ny, ny)], dst_ref=r1.at[o], send_sem=s1_sem.at[o],
            recv_sem=q1_sem.at[o], device_id=(to, gy), device_id_type=MESH)
        c.start()
        stage1.append(c)
        sent.append(c)

    inner(backward_row, 0, a1, EXCHANGES - 1, None)

    for c in stage1:
        c.wait_recv()
    summed = g3[pl.ds(gx * ny, ny)]
    for o in range(1, nx):
        summed = summed + r1[o]
    s2[...] = summed
    stage2 = []
    for o in range(1, ny):
        to = lax.rem(gy + o, ny)
        c = pltpu.make_async_remote_copy(
            src_ref=s2.at[to], dst_ref=r2.at[o], send_sem=s2_sem.at[o],
            recv_sem=q2_sem.at[o], device_id=(gx, to), device_id_type=MESH)
        c.start()
        stage2.append(c)
        sent.append(c)

    rim(backward_row, 0, a1, EXCHANGES - 1)

    for c in stage2:
        c.wait_recv()
    whole = s2[gy]
    for o in range(1, ny):
        whole = whole + r2[o]
    gout[...] = whole + pltpu.roll(whole, LANES - slots, 1)
    for c in sent:
        c.wait_send()


def shards(
    nx, ny,
    saved_fractions, adjoint_seed, slot_ids, active_counts, mobility, owner_pos, saved_instant
):
    slots, depth, rows, cols = saved_fractions.shape
    grains = mobility.shape[0]
    ndev = nx * ny
    out_per = grains // ndev
    steps = jnp.arange(STEPS, dtype=jnp.float32)
    therm = 0.75 + 0.5 * jnp.cos(0.3 * (saved_instant[0].astype(jnp.float32) + steps))
    flat = slots * depth * rows
    block = pltpu.VMEM((rows, depth, slots, cols), jnp.float32)
    plane = pltpu.VMEM((rows, slots, cols), jnp.float32)
    per = LANES // (2 * depth)
    packs = 5
    assert rows == 4 * per
    dma = pltpu.SemaphoreType.DMA
    vmem = pl.BlockSpec(memory_space=pltpu.VMEM)
    adjoint, owned = pl.pallas_call(
        functools.partial(kernel, nx, ny, slots, depth, rows, out_per),
        out_shape=(
            jax.ShapeDtypeStruct((flat, cols), jnp.float32),
            jax.ShapeDtypeStruct((1, LANES), jnp.float32),
        ),
        in_specs=[pl.BlockSpec(memory_space=pltpu.SMEM)] + [vmem] * 6,
        out_specs=(vmem, vmem),
        scratch_shapes=[block] * 9 + [
            pltpu.VMEM((flat, cols), jnp.float32),
            pltpu.VMEM((rows + 2, slots, cols), jnp.int32),
            pltpu.VMEM((4, rows, slots, cols), jnp.int32),
            pltpu.VMEM((4, rows, slots, cols), jnp.float32),
            plane, plane,
            pltpu.VMEM((rows, slots, cols), jnp.int32),
            plane,
            pltpu.VMEM((slots * depth, slots * depth), jnp.bfloat16),
            pltpu.VMEM((EXCHANGES, 2, depth, slots, cols), jnp.float32),
            pltpu.VMEM((EXCHANGES, packs, slots, LANES), jnp.float32),
            pltpu.VMEM((EXCHANGES, 2, packs, slots, LANES), jnp.float32),
            pltpu.VMEM((EXCHANGES, packs * per, slots, LANES), jnp.float32),
            pltpu.VMEM((EXCHANGES, packs * per, slots, LANES), jnp.float32),
            pltpu.VMEM((slots, LANES), jnp.int32),
            pltpu.VMEM((2, slots, LANES), jnp.int32),
            pltpu.VMEM((2, slots, LANES), jnp.int32),
            pltpu.VMEM((ndev, LANES), jnp.float32),
            pltpu.VMEM((ndev, 1, LANES), jnp.float32),
            pltpu.VMEM((nx, ny, 1, LANES), jnp.float32),
            pltpu.VMEM((ny, 1, LANES), jnp.float32),
            pltpu.VMEM((ny, 1, LANES), jnp.float32),
            dma((EXCHANGES, 2)), dma((EXCHANGES, 2)),
            dma((EXCHANGES, 3, 2)), dma((EXCHANGES, 3, 2)),
            dma((4,)), dma((4,)),
            dma((nx,)), dma((nx,)), dma((ny,)), dma((ny,)),
        ],
        compiler_params=pltpu.CompilerParams(
            collective_id=0, has_side_effects=True, vmem_limit_bytes=48 * 1024 * 1024
        ),
    )(
        therm,
        saved_fractions.reshape(flat, cols),
        adjoint_seed.reshape(flat, cols),
        slot_ids.reshape(slots * rows, cols),
        active_counts,
        mobility.reshape(grains // LANES, LANES),
        owner_pos.reshape(grains // LANES, LANES),
    )
    return adjoint.reshape(saved_fractions.shape), owned[0, :out_per]


def solution(mesh):
    placed = (
        P(None, None, "gx", "gy"),
        P(None, None, "gx", "gy"),
        P(None, "gx", "gy"),
        P("gx", "gy"),
        P(),
        P(),
        P(),
    )
    return jax.shard_map(
        functools.partial(shards, mesh.shape["gx"], mesh.shape["gy"]),
        mesh=mesh,
        in_specs=placed,
        out_specs=(P(None, None, "gx", "gy"), P(("gx", "gy"))),
        check_vma=False,
    )
```
